32 devices in a mesh: blk: 16 (over z, y, x), rep: 2 (over core).
Axes of the slice: x: 2, y: 2, z: 4, core: 2. Of those that a mesh axis runs over, the one named last changes fastest.
Arguments:
- features: bfloat16 [4096, 256], P(('blk', 'rep')), may hold values from -6 to 6
- degrees: int32 [4096], P(('blk', 'rep')), may hold values from 4 to 64
- tile_values: bfloat16 [32, 4, 2, 128, 128], P(('blk', 'rep')), may hold values from 0 to 1
- tile_rows: int32 [32, 4, 2], P(('blk', 'rep')), may hold values from 0 to 1, as said below
- tile_counts: int32 [32, 4], P(('blk', 'rep')), may hold values from 1 to 2, as said below
- weight: bfloat16 [256, 256], replicated, may hold values from -0.375 to 0.375
- cotangent: bfloat16 [4096, 256], P(('blk', 'rep')), may hold values from -6 to 6
Outputs:
- activations: bfloat16 [4096, 256], P(('blk', 'rep'))
- grad_weight: float32 [256, 256], replicated
- grad_features: bfloat16 [4096, 256], P(('blk', 'rep'))
The draws below stay inside these ranges and needn't reach their ends.
Inputs may be any that keep to these rules, and one draw needn't show every extreme that they name: `tile_rows`: the 2 slots of one owner and distance name the 2 row blocks of its slab, each once. Only the first tile_counts[o, s] slots of owner o and distance s are live. In every draw some slab has all 2 slots live at every distance for every owner in it.
All inputs are finite; a program needn't handle non-finite values.
Results may differ from the reference program's by a relative error of at most 0.0077.
Values may be sent and summed in bfloat16 or wider, within the bound.
A program may use at most 64 MiB of HBM per device.

```python
import math
import jax
import jax.numpy as jnp
from jax import lax

F = 256
BS = 128
ROWS_DEV = 128
SPAN = 4
CAP = 2
NODES = 4096
N_BLK = 16
N_REP = 2


def draw_tile_rows(key, part):
    scores = jax.random.randint(key, (N_BLK * N_REP, SPAN, CAP), 0, 2 ** 20)
    scores = scores * CAP + jnp.arange(CAP, dtype=jnp.int32)
    return jnp.argsort(scores, axis=-1, stable=True).astype(jnp.int32)


def draw_tile_counts(key, part):
    heavy_key = jax.random.fold_in(key, 11)
    pick_key = jax.random.fold_in(key, 12)
    light_key = jax.random.fold_in(key, 13)
    heavy_set = jax.random.randint(heavy_key, (N_BLK,), 0, 8) == 0
    chosen = jax.random.randint(pick_key, (), 0, N_BLK)
    heavy_set = heavy_set | (jnp.arange(N_BLK) == chosen)
    light_counts = jax.random.randint(light_key, (N_BLK * N_REP, SPAN), 1, CAP // 4 + 2)
    owner_index = jnp.arange(N_BLK * N_REP) // N_REP
    return jnp.where(heavy_set[owner_index][:, None], CAP, light_counts).astype(jnp.int32)


def with_ends(entries, own_key, low, largest):
    longest = entries.shape.index(max(entries.shape))
    spots = []
    for shift in (0, 1):
        where = [jax.random.randint(jax.random.fold_in(own_key, axis), (), 0, length) for axis, length in enumerate(entries.shape)]
        where[longest] = (where[longest] + shift) % entries.shape[longest]
        spots.append(tuple(where))
    return entries.at[spots[0]].set(low).at[spots[1]].set(largest)


def block_levels(key, dims, shards, least, top_value):
    gain, own = 1.0, jax.random.fold_in(key, 6)
    for dim, blocks in shards:
        draws = jnp.exp(jax.random.uniform(jax.random.fold_in(own, dim), (blocks,), jnp.float32, least / len(shards), top_value / len(shards)))
        gain = gain * jnp.repeat(draws, dims[dim] // blocks).reshape([-1 if axis == dim else 1 for axis in range(len(dims))])
    return gain


def normal_values(stream_key, dims, deviation, reach, split=(), held_as=jnp.bfloat16):
    gain = block_levels(stream_key, dims, split, -0.22, 0.18) if split else 1.0
    drawn = jax.random.normal(stream_key, dims, jnp.float32) * deviation * gain
    return jnp.minimum(jnp.maximum(drawn, -reach), reach).astype(held_as)


def setup_inputs(seed: int = 0) -> dict:
    seeds = jax.random.split(jax.random.key(seed), 8)
    features = normal_values(seeds[0], (NODES, F), 1.0, 6.0, ((0, 32),))
    degrees = with_ends(jax.random.randint(seeds[1], (NODES,), 4, 65), jax.random.fold_in(seeds[1], 1), 4, 64).astype(jnp.int32)
    tile_values = jnp.clip(1.0 * jax.random.uniform(seeds[2], (N_BLK * N_REP, SPAN, CAP, BS, ROWS_DEV), jnp.float32) ** block_levels(seeds[2], (N_BLK * N_REP, SPAN, CAP, BS, ROWS_DEV), ((0, 32),), -0.2, 0.2), 0.0, 1.0).astype(jnp.bfloat16)
    tile_rows = draw_tile_rows(jax.random.fold_in(seeds[7], 71), 0)
    tile_counts = draw_tile_counts(jax.random.fold_in(seeds[7], 71), 0)
    weight = normal_values(seeds[5], (F, F), F ** -0.5, 0.375)
    cotangent = normal_values(seeds[6], (NODES, F), 1.0, 6.0, ((0, 32),))
    return {"features": features, "degrees": degrees, "tile_values": tile_values, "tile_rows": tile_rows, "tile_counts": tile_counts, "weight": weight, "cotangent": cotangent}


def reference(features, degrees, tile_values, tile_rows, tile_counts, weight, cotangent):
    inv_root = lax.rsqrt(degrees.astype(jnp.float32))[:, None]
    scaled = (features.astype(jnp.float32) * inv_root).astype(jnp.bfloat16)
    source_view = scaled.reshape(N_BLK, N_REP, ROWS_DEV, F).astype(jnp.float32)
    tile_view = tile_values.reshape(N_BLK, N_REP, SPAN, CAP, BS, ROWS_DEV)
    slot_ids = jnp.arange(CAP, dtype=jnp.int32)
    live_slots = (slot_ids[None, None, :] < tile_counts[:, :, None]).astype(jnp.float32)
    placement = (tile_rows[:, :, :, None] == slot_ids[None, None, None, :]).astype(jnp.float32) * live_slots[:, :, :, None]
    place_view = placement.reshape(N_BLK, N_REP, SPAN, CAP, CAP)
    distances = jnp.arange(SPAN, dtype=jnp.int32)

    def placed_tiles(distance):
        tile_now = lax.dynamic_index_in_dim(tile_view, distance, 2, keepdims=False).astype(jnp.float32)
        place_now = lax.dynamic_index_in_dim(place_view, distance, 2, keepdims=False)
        return jnp.einsum('brkm,brkij->brmij', place_now, tile_now, precision=lax.Precision.HIGHEST)

    def forward_step(total, distance):
        moved = jnp.roll(source_view, distance, axis=0)
        placed = placed_tiles(distance)
        return (total + jnp.einsum('brmij,brjf->brmif', placed, moved, precision=lax.Precision.HIGHEST), None)
    zero_total = jnp.zeros((N_BLK, N_REP, CAP, BS, F), jnp.float32)
    partial_sum, _ = lax.scan(forward_step, zero_total, distances)
    summed = lax.optimization_barrier(jnp.sum(partial_sum, axis=1)).reshape(NODES, F)
    aggregated = (summed * inv_root).astype(jnp.bfloat16)
    pre_act = jnp.dot(aggregated, weight, preferred_element_type=jnp.float32)
    sigma = jax.nn.sigmoid(pre_act)
    activations = (pre_act * sigma).astype(jnp.bfloat16)
    act_grad = (cotangent.astype(jnp.float32) * sigma * (1.0 + pre_act * (1.0 - sigma))).astype(jnp.bfloat16)
    local_weight = lax.dot_general(aggregated, act_grad, (((0,), (0,)), ((), ())), preferred_element_type=jnp.float32)
    grad_weight = local_weight / math.sqrt(NODES)
    back_grad = lax.dot_general(act_grad, weight, (((1,), (1,)), ((), ())), preferred_element_type=jnp.float32)
    back_scaled = (back_grad * inv_root).astype(jnp.bfloat16)
    slab_view = back_scaled.reshape(N_BLK, CAP, BS, F).astype(jnp.float32)

    def backward_step(total, distance):
        placed = placed_tiles(distance)
        local_part = jnp.einsum('brmij,bmif->brjf', placed, slab_view, precision=lax.Precision.HIGHEST)
        return (total + jnp.roll(local_part, -distance, axis=0), None)
    zero_back = jnp.zeros((N_BLK, N_REP, ROWS_DEV, F), jnp.float32)
    back_total, _ = lax.scan(backward_step, zero_back, distances)
    grad_features = (back_total.reshape(NODES, F) * inv_root).astype(jnp.bfloat16)
    return (activations, grad_weight, grad_features)
```

```python
import functools
import math

import jax
import jax.numpy as jnp
from jax import lax
from jax.experimental import pallas as pl
from jax.experimental.pallas import tpu as pltpu
from jax.sharding import PartitionSpec as P

F32 = jnp.float32
BF16 = jnp.bfloat16
MESH = pl.DeviceIdType.MESH
GROUP = 4


def dot(a, b, ca, cb):
    return lax.dot_general(a, b, (((ca,), (cb,)), ((), ())), preferred_element_type=F32)


def fused_kernel(dims, *refs):
    n_blk, n_rep, span, cap, bs, own, width, nodes, reduce_here = dims
    (feat_hbm, deg_hbm, tile_hbm, rows_hbm, counts_hbm, w_hbm, cot_hbm,
     act_hbm, gw_hbm, gf_hbm,
     feat, deg, tiles, rows_s, counts_s, weight, cot, scaled, source, adj, part,
     agg, act_all, gact, back, inv, bpart, bpart_in, gf, gwf, gwb, ring1, ring2, gw_all,
     load_sem, fwd_send, fwd_recv, rep_send, rep_recv, bwd_send, bwd_recv,
     r1_send, r1_recv, r2_send, r2_recv, r3_send, r3_recv, out_sem) = refs
    slab = cap * bs
    depth = n_blk // GROUP
    me = lax.axis_index("blk")
    core = lax.axis_index("rep")

    def at_distance(s):
        return lax.rem(me + s + n_blk, n_blk)

    def at_core(u):
        return lax.rem(core + u, n_rep)

    plane = (me // GROUP) * GROUP
    spot = lax.rem(me, GROUP)

    def in_plane(t):
        return plane + lax.rem(spot + t, GROUP)

    barrier = pltpu.get_barrier_semaphore()
    peers = [(at_distance(s), core) for d in range(1, span) for s in (d, -d)]
    peers += [(me, at_core(u)) for u in range(1, n_rep)]
    if reduce_here:
        peers += [(in_plane(t), at_core(u)) for t in range(1, GROUP) for u in range(n_rep)]
        peers += [(at_distance(GROUP * t), core) for t in range(1, depth)]
    for peer in peers:
        pl.semaphore_signal(barrier, inc=1, device_id=peer, device_id_type=MESH)

    def load(src, dst, i):
        copy = pltpu.make_async_copy(src, dst, load_sem.at[i])
        copy.start()
        return copy

    mine = pl.ds(pl.multiple_of(core * own, own), own)
    loads = [
        load(deg_hbm, deg.at[core], 0),
        load(feat_hbm, feat, 1),
        load(rows_hbm, rows_s, 2),
        load(counts_hbm, counts_s, 3),
        load(tile_hbm, tiles, 4),
        load(cot_hbm, cot.at[core], 5),
        load(w_hbm, weight, 6),
    ]
    loads[0].wait()
    loads[1].wait()

    def column(row):
        block = jnp.broadcast_to(lax.rsqrt(row.astype(F32)), (own, own)).T
        return jnp.concatenate([block] * (width // own), axis=1)

    scaled[...] = (feat[...].astype(F32) * column(deg[core])).astype(BF16)
    pl.semaphore_wait(barrier, len(peers))

    def remote(src, dst, send, recv, peer):
        copy = pltpu.make_async_remote_copy(
            src_ref=src, dst_ref=dst, send_sem=send, recv_sem=recv,
            device_id=peer, device_id_type=MESH)
        copy.start()
        return copy

    forward = [
        remote(scaled, source.at[s - 1], fwd_send.at[s - 1], fwd_recv.at[s - 1], (at_distance(s), core))
        for s in range(span - 1, 0, -1)
    ][::-1]
    loads[5].wait()
    early = []
    for u in range(1, n_rep):
        peer = (me, at_core(u))
        early.append(remote(deg.at[core], deg.at[core], rep_send.at[0, u - 1], rep_recv.at[0, u - 1], peer))
        early.append(remote(cot.at[core], cot.at[core], rep_send.at[1, u - 1], rep_recv.at[1, u - 1], peer))
    loads[2].wait()
    loads[3].wait()
    loads[4].wait()

    def arrange(s, m):
        slot = jnp.int32(0)
        for k in range(cap):
            slot = jnp.where(rows_s[0, s, k] == m, k, slot)
        tile = tiles[0, s, slot]
        live = jnp.broadcast_to(slot < counts_s[0, s], tile.shape)
        return jnp.where(live, tile, jnp.zeros_like(tile))

    if span * cap <= 16:
        for s in range(span):
            for m in range(cap):
                adj[s, m * bs:(m + 1) * bs, :] = arrange(s, m)
    else:
        def arrange_one(i, carry):
            s = i // cap
            m = lax.rem(i, cap)
            adj[s, pl.ds(pl.multiple_of(m * bs, bs), bs), :] = arrange(s, m)
            return carry
        lax.fori_loop(0, span * cap, arrange_one, 0)

    part[core] = dot(adj[0], scaled[...], 1, 0)
    for s in range(1, span):
        forward[s - 1].wait_recv()
        part[core] += dot(adj[s], source[s - 1], 1, 0)
    exchange = [
        remote(part.at[core], part.at[core], rep_send.at[2, u - 1], rep_recv.at[2, u - 1], (me, at_core(u)))
        for u in range(1, n_rep)
    ]
    loads[6].wait()
    for copy in early:
        copy.wait_recv()
    for r in range(n_rep):
        inv[r * own:(r + 1) * own, :] = column(deg[r])
    for copy in exchange:
        copy.wait_recv()
    total = part[0]
    for r in range(1, n_rep):
        total = total + part[r]
    inv_root = inv[...]
    aggregated = (total * inv_root).astype(BF16)
    agg[...] = aggregated
    pre_act = jnp.dot(aggregated, weight[...], preferred_element_type=F32)
    sigma = jax.nn.sigmoid(pre_act)
    act_all[...] = (pre_act * sigma).astype(BF16)
    seed = cot[...].reshape(slab, width).astype(F32)
    act_grad = (seed * sigma * (1.0 + pre_act * (1.0 - sigma))).astype(BF16)
    gact[...] = act_grad
    scale = 1.0 / math.sqrt(nodes)
    if reduce_here:
        cols = width // n_rep
        piece = cols // GROUP
        half = agg[:, pl.ds(pl.multiple_of(core * cols, cols), cols)]
        local_weight = dot(half, act_grad, 0, 0) * scale
        gwf[...] = local_weight
        gwb[...] = local_weight.astype(BF16)
        first = []
        for t in range(1, GROUP):
            rows = pl.ds(pl.multiple_of(lax.rem(spot + t, GROUP) * piece, piece), piece)
            first.append(remote(gwb.at[rows], ring1.at[t - 1], r1_send.at[t - 1], r1_recv.at[t - 1],
                                (in_plane(t), core)))
    else:
        gwf[...] = dot(agg[mine, :], gact[mine, :], 0, 0) * scale
    back[...] = (dot(gact[...], weight[...], 1, 1) * inv_root).astype(BF16)
    backward = []
    for s in range(1, span):
        bpart[s - 1] = dot(adj[s], back[...], 0, 0).astype(BF16)
        backward.append(remote(bpart.at[s - 1], bpart_in.at[s - 1], bwd_send.at[s - 1], bwd_recv.at[s - 1],
                               (at_distance(-s), core)))
    outs = [pltpu.make_async_copy(act_all.at[mine], act_hbm, out_sem.at[0])]
    outs[0].start()
    own_back = dot(adj[0], back[...], 0, 0)
    if reduce_here:
        own_rows = pl.ds(pl.multiple_of(spot * piece, piece), piece)
        reduced = gwf[own_rows, :]
        for t in range(1, GROUP):
            first[t - 1].wait_recv()
            reduced = reduced + ring1[t - 1].astype(F32)
        level = me // GROUP
        ring2[level] = reduced.astype(BF16)
        second = [
            remote(ring2.at[level], ring2.at[level], r2_send.at[t - 1], r2_recv.at[t - 1],
                   (at_distance(GROUP * t), core))
            for t in range(1, depth)
        ]
        for copy in second:
            copy.wait_recv()
        whole = ring2[0].astype(F32)
        for t in range(1, depth):
            whole = whole + ring2[t].astype(F32)
        final_rows = pl.ds(pl.multiple_of(core * cols + spot * piece, piece), piece)
        gw_all[final_rows, :] = whole.astype(BF16)
        third = []
        for t in range(GROUP):
            for u in range(n_rep):
                if t or u:
                    i = t * n_rep + u - 1
                    third.append(remote(gw_all.at[final_rows], gw_all.at[final_rows], r3_send.at[i],
                                        r3_recv.at[i], (in_plane(t), at_core(u))))
    for s in range(1, span):
        backward[s - 1].wait_recv()
        own_back = own_back + bpart_in[s - 1].astype(F32)
    gf[...] = (own_back * inv[mine, :]).astype(BF16)
    outs.append(pltpu.make_async_copy(gf, gf_hbm, out_sem.at[1]))
    outs[1].start()
    if reduce_here:
        for copy in third:
            copy.wait_recv()
        outs.append(pltpu.make_async_copy(gw_all, gw_hbm, out_sem.at[2]))
    else:
        outs.append(pltpu.make_async_copy(gwf, gw_hbm, out_sem.at[2]))
    outs[2].start()
    sent = forward + early + exchange + backward
    if reduce_here:
        sent += first + second + third
    for copy in sent:
        copy.wait_send()
    for copy in outs:
        copy.wait()


def per_device(n_blk, n_rep, features, degrees, tile_values, tile_rows, tile_counts, weight, cotangent):
    own, width = features.shape
    _, span, cap, bs, _ = tile_values.shape
    nodes = own * n_blk * n_rep
    slab = cap * bs
    cols = width // n_rep
    reduce_here = n_blk % GROUP == 0 and n_blk // GROUP <= 4 and cols % 128 == 0
    piece = cols // GROUP
    depth = n_blk // GROUP
    dims = (n_blk, n_rep, span, cap, bs, own, width, nodes, reduce_here)
    gw_rows = cols if reduce_here else width
    dma = pltpu.SemaphoreType.DMA
    scratch = [
        pltpu.VMEM((own, width), BF16),
        pltpu.VMEM((n_rep, 1, own), jnp.int32),
        pltpu.VMEM(tile_values.shape, BF16),
        pltpu.SMEM(tile_rows.shape, jnp.int32),
        pltpu.SMEM(tile_counts.shape, jnp.int32),
        pltpu.VMEM((width, width), BF16),
        pltpu.VMEM((n_rep, own, width), BF16),
        pltpu.VMEM((own, width), BF16),
        pltpu.VMEM((span - 1, own, width), BF16),
        pltpu.VMEM((span, slab, bs), BF16),
        pltpu.VMEM((n_rep, slab, width), F32),
        pltpu.VMEM((slab, width), BF16),
        pltpu.VMEM((slab, width), BF16),
        pltpu.VMEM((slab, width), BF16),
        pltpu.VMEM((slab, width), BF16),
        pltpu.VMEM((slab, width), F32),
        pltpu.VMEM((span - 1, own, width), BF16),
        pltpu.VMEM((span - 1, own, width), BF16),
        pltpu.VMEM((own, width), BF16),
        pltpu.VMEM((gw_rows, width), F32),
        pltpu.VMEM((gw_rows, width), BF16),
        pltpu.VMEM((GROUP - 1, max(piece, 16), width), BF16),
        pltpu.VMEM((max(depth, 1), max(piece, 16), width), BF16),
        pltpu.VMEM((width, width), BF16),
        dma((7,)),
        dma((span - 1,)), dma((span - 1,)),
        dma((3, n_rep - 1)), dma((3, n_rep - 1)),
        dma((span - 1,)), dma((span - 1,)),
        dma((GROUP - 1,)), dma((GROUP - 1,)),
        dma((max(depth - 1, 1),)), dma((max(depth - 1, 1),)),
        dma((GROUP * n_rep - 1,)), dma((GROUP * n_rep - 1,)),
        dma((3,)),
    ]
    anywhere = pl.BlockSpec(memory_space=pl.ANY)
    activations, grad_weight, grad_features = pl.pallas_call(
        functools.partial(fused_kernel, dims),
        out_shape=(
            jax.ShapeDtypeStruct((own, width), BF16),
            jax.ShapeDtypeStruct((width, width), BF16 if reduce_here else F32),
            jax.ShapeDtypeStruct((own, width), BF16),
        ),
        in_specs=[anywhere] * 7,
        out_specs=(anywhere,) * 3,
        scratch_shapes=scratch,
        compiler_params=pltpu.CompilerParams(
            collective_id=0, has_side_effects=True, vmem_limit_bytes=48 * 1024 * 1024),
    )(features, degrees.reshape(1, own), tile_values, tile_rows, tile_counts, weight, cotangent)
    if reduce_here:
        grad_weight = grad_weight.astype(F32)
    else:
        grad_weight = lax.psum(grad_weight, ("blk", "rep"))
    return (activations, grad_weight, grad_features)


def solution(mesh):
    placed = (
        P(("blk", "rep"), None),
        P(("blk", "rep")),
        P(("blk", "rep"), None, None, None, None),
        P(("blk", "rep"), None, None),
        P(("blk", "rep"), None),
        P(),
        P(("blk", "rep"), None),
    )
    return jax.shard_map(
        functools.partial(per_device, mesh.shape["blk"], mesh.shape["rep"]),
        mesh=mesh,
        in_specs=placed,
        out_specs=(P(("blk", "rep"), None), P(), P(("blk", "rep"), None)),
        check_vma=False,
    )
```

```python
import functools
import math

import jax
import jax.numpy as jnp
from jax import lax
from jax.experimental import pallas as pl
from jax.experimental.pallas import tpu as pltpu
from jax.sharding import PartitionSpec as P

F32 = jnp.float32
BF16 = jnp.bfloat16
MESH = pl.DeviceIdType.MESH
GROUP = 4


def dot(a, b, ca, cb):
    return lax.dot_general(a, b, (((ca,), (cb,)), ((), ())), preferred_element_type=F32)


def fused_kernel(dims, *refs):
    n_blk, n_rep, span, cap, bs, own, width, nodes, reduce_here = dims
    (feat_hbm, deg_hbm, tile_hbm, rows_hbm, counts_hbm, w_hbm, cot_hbm,
     act_out, gw_out, gf_out,
     feat, deg, tiles, rows_s, counts_s, weight, cot, scaled, source, adj, part,
     agg, act_all, gact, back, inv, bpart, bpart_in, gwf, gwb, ring1, ring2, gw_all,
     load_sem, fwd_send, fwd_recv, rep_send, rep_recv, bwd_send, bwd_recv,
     r1_send, r1_recv, r2_send, r2_recv, r3_send, r3_recv) = refs
    slab = cap * bs
    depth = n_blk // GROUP
    me = lax.axis_index("blk")
    core = lax.axis_index("rep")

    def at_distance(s):
        return lax.rem(me + s + n_blk, n_blk)

    def at_core(u):
        return lax.rem(core + u, n_rep)

    plane = (me // GROUP) * GROUP
    spot = lax.rem(me, GROUP)

    def in_plane(t):
        return plane + lax.rem(spot + t, GROUP)

    barrier = pltpu.get_barrier_semaphore()
    peers = [(at_distance(s), core) for d in range(1, span) for s in (d, -d)]
    peers += [(me, at_core(u)) for u in range(1, n_rep)]
    if reduce_here:
        peers += [(in_plane(t), at_core(u)) for t in range(1, GROUP) for u in range(n_rep)]
        peers += [(at_distance(GROUP * t), core) for t in range(1, depth)]
    for peer in peers:
        pl.semaphore_signal(barrier, inc=1, device_id=peer, device_id_type=MESH)

    def load(src, dst, i):
        copy = pltpu.make_async_copy(src, dst, load_sem.at[i])
        copy.start()
        return copy

    mine = pl.ds(pl.multiple_of(core * own, own), own)
    loads = [
        load(deg_hbm, deg.at[core], 0),
        load(feat_hbm, feat, 1),
        load(rows_hbm, rows_s, 2),
        load(counts_hbm, counts_s, 3),
        load(tile_hbm, tiles, 4),
        load(cot_hbm, cot.at[core], 5),
        load(w_hbm, weight, 6),
    ]
    loads[0].wait()
    loads[1].wait()

    def column(row):
        block = jnp.broadcast_to(lax.rsqrt(row.astype(F32)), (own, own)).T
        return jnp.concatenate([block] * (width // own), axis=1)

    scaled[...] = (feat[...].astype(F32) * column(deg[core])).astype(BF16)
    pl.semaphore_wait(barrier, len(peers))

    def remote(src, dst, send, recv, peer):
        copy = pltpu.make_async_remote_copy(
            src_ref=src, dst_ref=dst, send_sem=send, recv_sem=recv,
            device_id=peer, device_id_type=MESH)
        copy.start()
        return copy

    forward = [
        remote(scaled, source.at[s - 1], fwd_send.at[s - 1], fwd_recv.at[s - 1], (at_distance(s), core))
        for s in range(span - 1, 0, -1)
    ][::-1]
    loads[5].wait()
    early = []
    for u in range(1, n_rep):
        peer = (me, at_core(u))
        early.append(remote(deg.at[core], deg.at[core], rep_send.at[0, u - 1], rep_recv.at[0, u - 1], peer))
        early.append(remote(cot.at[core], cot.at[core], rep_send.at[1, u - 1], rep_recv.at[1, u - 1], peer))
    loads[2].wait()
    loads[3].wait()
    loads[4].wait()

    def arrange(s, m):
        slot = jnp.int32(0)
        for k in range(cap):
            slot = jnp.where(rows_s[0, k, s] == m, k, slot)
        tile = tiles[0, s, slot]
        live = jnp.broadcast_to(slot < counts_s[0, s], tile.shape)
        return jnp.where(live, tile, jnp.zeros_like(tile))

    if span * cap <= 16:
        for s in range(span):
            for m in range(cap):
                adj[s, m * bs:(m + 1) * bs, :] = arrange(s, m)
    else:
        def arrange_one(i, carry):
            s = i // cap
            m = lax.rem(i, cap)
            adj[s, pl.ds(pl.multiple_of(m * bs, bs), bs), :] = arrange(s, m)
            return carry
        lax.fori_loop(0, span * cap, arrange_one, 0)

    part[core] = dot(adj[0], scaled[...], 1, 0)
    for s in range(1, span):
        forward[s - 1].wait_recv()
        part[core] += dot(adj[s], source[s - 1], 1, 0)
    exchange = [
        remote(part.at[core], part.at[core], rep_send.at[2, u - 1], rep_recv.at[2, u - 1], (me, at_core(u)))
        for u in range(1, n_rep)
    ]
    loads[6].wait()
    for copy in early:
        copy.wait_recv()
    for r in range(n_rep):
        inv[r * own:(r + 1) * own, :] = column(deg[r])
    for copy in exchange:
        copy.wait_recv()
    total = part[0]
    for r in range(1, n_rep):
        total = total + part[r]
    inv_root = inv[...]
    aggregated = (total * inv_root).astype(BF16)
    agg[...] = aggregated
    pre_act = jnp.dot(aggregated, weight[...], preferred_element_type=F32)
    sigma = jax.nn.sigmoid(pre_act)
    act_all[...] = (pre_act * sigma).astype(BF16)
    seed = cot[...].reshape(slab, width).astype(F32)
    act_grad = (seed * sigma * (1.0 + pre_act * (1.0 - sigma))).astype(BF16)
    gact[...] = act_grad
    scale = 1.0 / math.sqrt(nodes)
    if reduce_here:
        cols = width // n_rep
        piece = cols // GROUP
        half = agg[:, pl.ds(pl.multiple_of(core * cols, cols), cols)]
        local_weight = dot(half, act_grad, 0, 0) * scale
        gwf[...] = local_weight
        gwb[...] = local_weight.astype(BF16)
        first = []
        for t in range(1, GROUP):
            rows = pl.ds(pl.multiple_of(lax.rem(spot + t, GROUP) * piece, piece), piece)
            first.append(remote(gwb.at[rows], ring1.at[t - 1], r1_send.at[t - 1], r1_recv.at[t - 1],
                                (in_plane(t), core)))
    else:
        gwf[...] = dot(agg[mine, :], gact[mine, :], 0, 0) * scale
    back[...] = (dot(gact[...], weight[...], 1, 1) * inv_root).astype(BF16)
    backward = []
    for s in range(1, span):
        bpart[s - 1] = dot(adj[s], back[...], 0, 0).astype(BF16)
        backward.append(remote(bpart.at[s - 1], bpart_in.at[s - 1], bwd_send.at[s - 1], bwd_recv.at[s - 1],
                               (at_distance(-s), core)))
    act_out[...] = act_all[mine, :]
    own_back = dot(adj[0], back[...], 0, 0)
    if reduce_here:
        own_rows = pl.ds(pl.multiple_of(spot * piece, piece), piece)
        reduced = gwf[own_rows, :]
        for t in range(1, GROUP):
            first[t - 1].wait_recv()
            reduced = reduced + ring1[t - 1].astype(F32)
        level = me // GROUP
        ring2[level] = reduced.astype(BF16)
        second = [
            remote(ring2.at[level], ring2.at[level], r2_send.at[t - 1], r2_recv.at[t - 1],
                   (at_distance(GROUP * t), core))
            for t in range(1, depth)
        ]
        for copy in second:
            copy.wait_recv()
        whole = ring2[0].astype(F32)
        for t in range(1, depth):
            whole = whole + ring2[t].astype(F32)
        final_rows = pl.ds(pl.multiple_of(core * cols + spot * piece, piece), piece)
        gw_all[final_rows, :] = whole.astype(BF16)
        third = []
        for t in range(GROUP):
            for u in range(n_rep):
                if t or u:
                    i = t * n_rep + u - 1
                    third.append(remote(gw_all.at[final_rows], gw_all.at[final_rows], r3_send.at[i],
                                        r3_recv.at[i], (in_plane(t), at_core(u))))
    for s in range(1, span):
        backward[s - 1].wait_recv()
        own_back = own_back + bpart_in[s - 1].astype(F32)
    gf_out[...] = (own_back * inv[mine, :]).astype(BF16)
    if reduce_here:
        for copy in third:
            copy.wait_recv()
        gw_out[...] = gw_all[...].astype(F32)
    else:
        gw_out[...] = gwf[...]
    sent = forward + early + exchange + backward
    if reduce_here:
        sent += first + second + third
    for copy in sent:
        copy.wait_send()


def store_kernel(*refs):
    sources, targets, sem = refs[:3], refs[3:6], refs[6]
    copies = [pltpu.make_async_copy(sources[i], targets[i], sem.at[i]) for i in range(3)]
    for copy in copies:
        copy.start()
    for copy in copies:
        copy.wait()


def per_device(n_blk, n_rep, features, degrees, tile_values, tile_rows, tile_counts, weight, cotangent):
    own, width = features.shape
    _, span, cap, bs, _ = tile_values.shape
    nodes = own * n_blk * n_rep
    slab = cap * bs
    cols = width // n_rep
    reduce_here = n_blk % GROUP == 0 and n_blk // GROUP <= 4 and cols % 128 == 0
    piece = cols // GROUP
    depth = n_blk // GROUP
    dims = (n_blk, n_rep, span, cap, bs, own, width, nodes, reduce_here)
    gw_rows = cols if reduce_here else width
    dma = pltpu.SemaphoreType.DMA
    scratch = [
        pltpu.VMEM((own, width), BF16),
        pltpu.VMEM((n_rep, 1, own), jnp.int32),
        pltpu.VMEM(tile_values.shape, BF16),
        pltpu.SMEM((1, cap, span), jnp.int32),
        pltpu.SMEM(tile_counts.shape, jnp.int32),
        pltpu.VMEM((width, width), BF16),
        pltpu.VMEM((n_rep, own, width), BF16),
        pltpu.VMEM((own, width), BF16),
        pltpu.VMEM((span - 1, own, width), BF16),
        pltpu.VMEM((span, slab, bs), BF16),
        pltpu.VMEM((n_rep, slab, width), F32),
        pltpu.VMEM((slab, width), BF16),
        pltpu.VMEM((slab, width), BF16),
        pltpu.VMEM((slab, width), BF16),
        pltpu.VMEM((slab, width), BF16),
        pltpu.VMEM((slab, width), F32),
        pltpu.VMEM((span - 1, own, width), BF16),
        pltpu.VMEM((span - 1, own, width), BF16),
        pltpu.VMEM((gw_rows, width), F32),
        pltpu.VMEM((gw_rows, width), BF16),
        pltpu.VMEM((GROUP - 1, max(piece, 16), width), BF16),
        pltpu.VMEM((max(depth, 1), max(piece, 16), width), BF16),
        pltpu.VMEM((width, width), BF16),
        dma((7,)),
        dma((span - 1,)), dma((span - 1,)),
        dma((3, n_rep - 1)), dma((3, n_rep - 1)),
        dma((span - 1,)), dma((span - 1,)),
        dma((GROUP - 1,)), dma((GROUP - 1,)),
        dma((max(depth - 1, 1),)), dma((max(depth - 1, 1),)),
        dma((GROUP * n_rep - 1,)), dma((GROUP * n_rep - 1,)),
    ]
    anywhere = pl.BlockSpec(memory_space=pl.ANY)
    in_vmem = pl.BlockSpec(memory_space=pltpu.VMEM)
    in_hbm = pl.BlockSpec(memory_space=pltpu.HBM)
    activations, grad_weight, grad_features = pl.pallas_call(
        functools.partial(fused_kernel, dims),
        out_shape=(
            jax.ShapeDtypeStruct((own, width), BF16),
            jax.ShapeDtypeStruct((width, width), F32),
            jax.ShapeDtypeStruct((own, width), BF16),
        ),
        in_specs=[in_hbm] * 7,
        out_specs=(in_vmem,) * 3,
        scratch_shapes=scratch,
        compiler_params=pltpu.CompilerParams(
            collective_id=0, has_side_effects=True, vmem_limit_bytes=48 * 1024 * 1024),
    )(*[pltpu.with_memory_space_constraint(x, pltpu.HBM) for x in (
        features, degrees.reshape(1, own), tile_values, tile_rows.transpose(0, 2, 1),
        tile_counts, weight, cotangent)])
    activations, grad_weight, grad_features = pl.pallas_call(
        store_kernel,
        out_shape=(
            jax.ShapeDtypeStruct((own, width), BF16),
            jax.ShapeDtypeStruct((width, width), F32),
            jax.ShapeDtypeStruct((own, width), BF16),
        ),
        in_specs=[anywhere] * 3,
        out_specs=(in_hbm,) * 3,
        scratch_shapes=[dma((3,))],
    )(*[pltpu.with_memory_space_constraint(x, pltpu.VMEM) for x in (activations, grad_weight, grad_features)])
    if not reduce_here:
        grad_weight = lax.psum(grad_weight, ("blk", "rep"))
    return (activations, grad_weight, grad_features)


def solution(mesh):
    placed = (
        P(("blk", "rep"), None),
        P(("blk", "rep")),
        P(("blk", "rep"), None, None, None, None),
        P(("blk", "rep"), None, None),
        P(("blk", "rep"), None),
        P(),
        P(("blk", "rep"), None),
    )
    return jax.shard_map(
        functools.partial(per_device, mesh.shape["blk"], mesh.shape["rep"]),
        mesh=mesh,
        in_specs=placed,
        out_specs=(P(("blk", "rep"), None), P(), P(("blk", "rep"), None)),
        check_vma=False,
    )
```
